32 devices in a mesh: row: 4 (over y, x), col: 8 (over z, core).
Axes of the slice: x: 2, y: 2, z: 4, core: 2. Of those that a mesh axis runs over, the one named last changes fastest.
Arguments:
- pair_ints: bfloat16 [2048, 16384], P(None, ('row', 'col')), may hold values from -0.59765625 to 0.59765625
- denominators: float32 [2048], replicated, may hold values from 0.5 to 4
- lap_points: float32 [3], replicated, may hold values from 0.05 to 1.5
- lap_weights: float32 [3], replicated, may hold values from 0.2 to 1
Outputs:
- aux_matrices: float32 [3, 16384, 16384], P(None, 'row', 'col')
The draws below stay inside these ranges and needn't reach their ends.
All inputs are finite; a program needn't handle non-finite values.
Results may differ from the reference program's by a relative error of at most 0.0027.
Values may be sent and summed in bfloat16 or wider, within the bound.
No kernel may reach another device: no remote copies, remote signals or barrier semaphores. Data moves between devices by JAX's collectives and lax.ppermute only.
A program may use at most 256 MiB of HBM per device.

```python
import math
import jax
import jax.numpy as jnp
from jax import lax

NAUX = 16384
R = 2048
NT = 3


def block_scale(own_key, shape, shards, smallest, high):
    factor_of, own = 1.0, jax.random.fold_in(own_key, 6)
    for dim, blocks in shards:
        draws = jnp.exp(jax.random.uniform(jax.random.fold_in(own, dim), (blocks,), jnp.float32, smallest / len(shards), high / len(shards)))
        factor_of = factor_of * jnp.repeat(draws, shape[dim] // blocks).reshape([-1 if axis == dim else 1 for axis in range(len(shape))])
    return factor_of


def centred(key, extent, spread, reach, pieces=(), dtype=jnp.bfloat16):
    level = block_scale(key, extent, pieces, -0.22, 0.18) if pieces else 1.0
    entries = jax.random.normal(key, extent, jnp.float32) * spread * level
    return jnp.minimum(jnp.maximum(entries, -reach), reach).astype(dtype)


def setup_inputs(seed: int = 0) -> dict:
    streams_of = jax.random.split(jax.random.key(seed), 5)
    pair_ints = centred(streams_of[0], (R, NAUX), 0.08, 0.59765625, ((1, 32),))
    denominators = jnp.clip(jax.random.uniform(streams_of[1], (R,), jnp.float32, 0.5, 4.0), 0.5, 4.0)
    lap_points = jnp.clip(jnp.exp(jax.random.uniform(streams_of[2], (NT,), jnp.float32, math.log(0.05), math.log(1.5))), 0.05, 1.5)
    lap_weights = jnp.clip(jnp.exp(jax.random.uniform(streams_of[3], (NT,), jnp.float32, math.log(0.2), math.log(1.0))), 0.2, 1.0)
    return {"pair_ints": pair_ints, "denominators": denominators, "lap_points": lap_points, "lap_weights": lap_weights}


def reference(pair_ints, denominators, lap_points, lap_weights):
    values = pair_ints.astype(jnp.float32)

    def single(inputs):
        point, weight = inputs
        factor = weight * jnp.exp(-point * denominators)
        weighted = (values * factor[:, None]).astype(jnp.bfloat16)
        weighted = lax.optimization_barrier(weighted).astype(jnp.float32)
        return jnp.dot(weighted.T, values, precision=lax.Precision.HIGHEST)

    return lax.map(single, (lap_points, lap_weights))
```

```python
import jax
import jax.numpy as jnp
from jax import lax
from jax.experimental import pallas as pl
from jax.experimental.pallas import tpu as pltpu
from jax.sharding import PartitionSpec as P

CHUNK = 512
SUB = 256
SLOTS = 3


def gemm_kernel(plan, offs_ref, fac_ref, *refs):
    n_rows, first, n_halves, groups, piece, hw, width, has_out, sub = plan
    refs = list(refs)
    row_refs = [refs.pop(0) for _ in range(n_rows)]
    col_refs = [[refs.pop(0) for _ in range(groups)] for _ in range(n_halves)]
    if has_out:
        refs.pop(0)
    out_ref = refs.pop(0)
    rows_v, cols_v, w_v, o_v, row_sem, col_sem, out_sem = refs
    nt, depth = fac_ref.shape
    kq = depth // groups
    per = CHUNK // hw
    per_half = groups // per
    chunks = n_halves * per_half
    subs = n_rows * piece // sub
    part = sub // chunks

    def row_copy(p):
        return pltpu.make_async_copy(row_refs[p], rows_v.at[pl.ds(p * piece, piece)], row_sem.at[p])

    def col_copies(h):
        out = []
        for g in range(groups):
            place = offs_ref[subs + g]
            for j in range(groups):
                i = lax.rem(place - j + groups, groups)
                c = h * per_half + i // per
                out.append(
                    pltpu.make_async_copy(
                        col_refs[h][g].at[j],
                        cols_v.at[c, pl.ds(pl.multiple_of(place * kq, kq), kq), pl.ds(pl.multiple_of(lax.rem(i, per) * hw, hw), hw)],
                        col_sem.at[h, g, j],
                    )
                )
        return out

    row_copy(0).start()
    for h in range(n_halves):
        for c in col_copies(h):
            c.start()
    for p in range(1, n_rows):
        row_copy(p).start()

    def weigh(slot, src, dst, count):
        x = rows_v[pl.ds(src, count), :].astype(jnp.float32)
        for t in range(nt):
            w_v[slot, pl.ds(t * sub + dst, count), :] = (x * fac_ref[pl.ds(t, 1), :]).astype(jnp.bfloat16)

    row_copy(0).wait()
    weigh(0, 0, 0, sub)
    for h in range(n_halves):
        for c in col_copies(h):
            c.wait()
    for p in range(1, n_rows):
        row_copy(p).wait()

    def out_copies(slot, s, n):
        h = n // per_half
        i0 = lax.rem(n, per_half) * per
        row0 = pl.multiple_of(offs_ref[s], sub)
        return [
            pltpu.make_async_copy(
                o_v.at[slot, :, :, pl.ds(e * hw, hw)],
                out_ref.at[:, pl.ds(row0, sub), pl.ds(pl.multiple_of((i0 + e) * width + (first + h) * hw, hw), hw)],
                out_sem.at[slot, e],
            )
            for e in range(per)
        ]

    total = subs * chunks

    def step(q, _):
        s, n = q // chunks, lax.rem(q, chunks)
        slot = lax.rem(q, SLOTS)
        cur = lax.rem(s, 2)

        @pl.when(q >= SLOTS)
        def _():
            for c in out_copies(slot, s, n):
                c.wait()

        nxt = jnp.minimum(s + 1, subs - 1)
        weigh(1 - cur, pl.multiple_of(nxt * sub + n * part, part), pl.multiple_of(n * part, part), part)
        res = jnp.dot(w_v[cur], cols_v[n], preferred_element_type=jnp.float32)
        o_v[slot] = res.reshape(nt, sub, CHUNK)
        for c in out_copies(slot, s, n):
            c.start()
        return 0

    lax.fori_loop(0, total, step, 0)
    for q in range(max(0, total - SLOTS), total):
        for c in out_copies(q % SLOTS, q // chunks, q % chunks):
            c.wait()


def gemm(factors, rows, row_offs, first, halves, places, out, out_shape, width):
    nt, depth = factors.shape
    piece = rows[0].shape[0]
    groups = len(halves[0])
    hw = halves[0][0].shape[2]
    sub = min(SUB, piece)
    offs = [o + k * sub for o in row_offs for k in range(piece // sub)] + list(places)
    offs = jnp.stack([jnp.asarray(o, jnp.int32) for o in offs])
    chunks = len(halves) * groups * hw // CHUNK
    plan = (len(rows), first, len(halves), groups, piece, hw, width, out is not None, sub)
    args = [factors, *rows, *[a for h in halves for a in h]]
    hbm = pl.BlockSpec(memory_space=pl.ANY)
    in_specs = [pl.BlockSpec(memory_space=pltpu.VMEM)] + [hbm] * (len(args) - 1)
    aliases = {}
    if out is not None:
        aliases = {len(args) + 1: 0}
        args.append(out)
        in_specs.append(hbm)
    m, n = len(rows) * piece, len(halves) * groups * hw
    return pl.pallas_call(
        lambda *refs: gemm_kernel(plan, *refs),
        out_shape=jax.ShapeDtypeStruct(out_shape, jnp.float32),
        grid_spec=pltpu.PrefetchScalarGridSpec(
            num_scalar_prefetch=1,
            grid=(),
            in_specs=in_specs,
            out_specs=hbm,
            scratch_shapes=[
                pltpu.VMEM((m, depth), jnp.bfloat16),
                pltpu.VMEM((chunks, depth, CHUNK), jnp.bfloat16),
                pltpu.VMEM((2, nt * sub, depth), jnp.bfloat16),
                pltpu.VMEM((SLOTS, nt, sub, CHUNK), jnp.float32),
                pltpu.SemaphoreType.DMA((len(rows),)),
                pltpu.SemaphoreType.DMA((len(halves), groups, groups)),
                pltpu.SemaphoreType.DMA((SLOTS, CHUNK // hw)),
            ],
        ),
        input_output_aliases=aliases,
        compiler_params=pltpu.CompilerParams(vmem_limit_bytes=48 * 1024 * 1024),
        cost_estimate=pl.CostEstimate(
            flops=2 * nt * m * n * depth,
            bytes_accessed=4 * nt * m * n + 2 * depth * (m + n),
            transcendentals=0,
        ),
    )(offs, *args)


def solution(mesh):
    R, C = mesh.shape["row"], mesh.shape["col"]
    Z = C // 2

    def on_device(pair_ints, denominators, lap_points, lap_weights):
        depth, width = pair_ints.shape
        r, u = lax.axis_index("row"), lax.axis_index("col")
        z, core = u // 2, lax.rem(u, 2)
        factors = lap_weights[:, None] * jnp.exp(-lap_points[:, None] * denominators[None, :])
        nt = factors.shape[0]
        kq = depth // R
        n_halves = 2 if width % 256 == 0 else 1
        hw = width // n_halves

        flat = r * C + u
        own = []
        for h in range(n_halves):
            pieces = []
            for j in range(R):
                q = lax.rem(lax.rem(flat, R) + j, R)
                piece = lax.dynamic_slice(pair_ints, (q * kq, h * hw), (kq, hw))
                perm = [(f, ((f % R + j) % R) * C + f // R) for f in range(R * C)]
                pieces.append(lax.ppermute(piece, ("row", "col"), perm))
            own.append(jnp.stack(pieces))

        def row_perm(x, e):
            return lax.ppermute(x, "row", [(a, a ^ e) for a in range(R)])

        halves = [[own[h]] + [row_perm(own[h], e) for e in range(1, R)] for h in range(n_halves)]
        places = [r ^ e for e in range(R)]

        def col_perm(x, pairs):
            return lax.ppermute(x, "col", [(2 * a + k, 2 * b + k) for a, b in pairs for k in range(2)])

        def swap(x):
            return lax.ppermute(x, "col", [(a, a ^ 1) for a in range(C)])

        mine = pair_ints.T
        arrivals = []
        if Z == 4:
            up = col_perm(mine, [((a + 1) % Z, a) for a in range(Z)])
            down = col_perm(mine, [((a - 1) % Z, a) for a in range(Z)])
            fwd = jnp.where(z == 1, up, jnp.where(z == 2, down, mine))
            pairs = [(1, 0), (2, 3), (3, 1), (0, 2)]
            m2 = width // 2
            arrivals = [
                (up, lax.rem(z + 1, Z), 0),
                (down, lax.rem(z + 3, Z), 0),
                (col_perm(fwd[:m2], pairs), lax.rem(z + 2, Z), 0),
                (col_perm(fwd[m2:], pairs), lax.rem(z + 2, Z), m2),
            ]
        else:
            for d in range(1, Z):
                arrivals.append((col_perm(mine, [((a + d) % Z, a) for a in range(Z)]), lax.rem(z + d, Z), 0))

        out_shape = (nt, C * width, R * width)

        def block(x, where, extra, first, hs, out):
            offs = [(2 * where + core) * width + extra, (2 * where + 1 - core) * width + extra]
            return gemm(factors, [x[0], x[1]], offs, first, hs, places, out, out_shape, width)

        pair = (mine, swap(mine))
        out = None
        for h in range(n_halves):
            out = block(pair, z, 0, h, [halves[h]], out)
        for x, where, extra in arrivals:
            out = block((x, swap(x)), where, extra, 0, halves, out)
        return out

    in_specs = (P(None, ("row", "col")), P(), P(), P())
    out_specs = P(None, "row", "col")
    return jax.shard_map(on_device, mesh=mesh, in_specs=in_specs, out_specs=out_specs, check_vma=False)
```

```python
import jax
import jax.numpy as jnp
from jax import lax
from jax.experimental import pallas as pl
from jax.experimental.pallas import tpu as pltpu
from jax.sharding import PartitionSpec as P

CHUNK = 512
SUB = 512
SLOTS = 3
COST = 2


def gemm_kernel(plan, offs_ref, fac_ref, *refs):
    n_rows, first, n_halves, groups, piece, hw, width, n_more, sub = plan
    refs = list(refs)
    row_refs = [refs.pop(0) for _ in range(n_rows)]
    col_refs = [[refs.pop(0) for _ in range(groups)] for _ in range(n_halves)]
    refs = refs[n_more:]
    out_ref, tok_ref = refs.pop(0), refs.pop(0)
    tok_ref[...] = jnp.zeros_like(tok_ref)
    rows_v, cols_v, w_v, o_v, row_sem, col_sem, out_sem = refs
    nt, depth = fac_ref.shape
    per = CHUNK // hw
    per_half = groups // per
    chunks = n_halves * per_half
    subs = n_rows * piece // sub
    part = sub // chunks

    def row_copy(p):
        return pltpu.make_async_copy(row_refs[p], rows_v.at[pl.ds(p * piece, piece)], row_sem.at[p])

    def col_copy(h, g, sem_h, sem_g):
        i = offs_ref[subs + g]
        return pltpu.make_async_copy(
            col_refs[h][g],
            cols_v.at[h * per_half + i // per, :, pl.ds(pl.multiple_of(lax.rem(i, per) * hw, hw), hw)],
            col_sem.at[sem_h, sem_g],
        )

    row_copy(0).start()
    for h in range(n_halves):
        for g in range(groups):
            col_copy(h, g, h, g).start()
    for p in range(1, n_rows):
        row_copy(p).start()

    def weigh(slot, src, dst, count):
        x = rows_v[pl.ds(src, count), :].astype(jnp.float32)
        for t in range(nt):
            w_v[slot, pl.ds(t * sub + dst, count), :] = (x * fac_ref[pl.ds(t, 1), :]).astype(jnp.bfloat16)

    row_copy(0).wait()
    weigh(0, 0, 0, sub)

    def out_copies(slot, s, n):
        h = n // per_half
        i0 = lax.rem(n, per_half) * per
        row0 = pl.multiple_of(offs_ref[s], sub)
        return [
            pltpu.make_async_copy(
                o_v.at[slot, :, :, pl.ds(e * hw, hw)],
                out_ref.at[:, pl.ds(row0, sub), pl.ds(pl.multiple_of((i0 + e) * width + (first + h) * hw, hw), hw)],
                out_sem.at[slot, e],
            )
            for e in range(per)
        ]

    total = subs * chunks

    def step(q, _):
        s, n = q // chunks, lax.rem(q, chunks)
        slot = lax.rem(q, SLOTS)
        cur = lax.rem(s, 2)

        @pl.when(s == 0)
        def _():
            h = n // per_half
            for e in range(per):
                g = offs_ref[subs + lax.rem(n, per_half) * per + e]
                col_copy(0, 0, h, g).wait()

        for p in range(1, n_rows):

            @pl.when((n == 0) & (s + 1 == p * (piece // sub)))
            def _():
                row_copy(p).wait()

        @pl.when(q >= SLOTS)
        def _():
            for c in out_copies(slot, s, n):
                c.wait()

        nxt = jnp.minimum(s + 1, subs - 1)
        weigh(1 - cur, pl.multiple_of(nxt * sub + n * part, part), pl.multiple_of(n * part, part), part)
        res = jnp.dot(w_v[cur], cols_v[n], preferred_element_type=jnp.float32)
        o_v[slot] = res.reshape(nt, sub, CHUNK)
        for c in out_copies(slot, s, n):
            c.start()
        return 0

    lax.fori_loop(0, total, step, 0)
    for q in range(max(0, total - SLOTS), total):
        for c in out_copies(q % SLOTS, q // chunks, q % chunks):
            c.wait()


def tie(x, *deps):
    hbm = pl.BlockSpec(memory_space=pl.ANY)
    return pl.pallas_call(
        lambda *refs: None,
        out_shape=jax.ShapeDtypeStruct(x.shape, x.dtype),
        in_specs=[hbm] * (1 + len(deps)),
        out_specs=hbm,
        input_output_aliases={0: 0},
        compiler_params=pltpu.CompilerParams(vmem_limit_bytes=48 * 1024 * 1024),
    )(x, *deps)


def gemm(factors, rows, row_offs, first, halves, places, out, out_shape, width, deps=()):
    nt, depth = factors.shape
    piece = rows[0].shape[0]
    groups = len(halves[0])
    hw = halves[0][0].shape[1]
    sub = min(SUB, piece)
    offs = [o + k * sub for o in row_offs for k in range(piece // sub)] + list(places)
    offs = jnp.stack([jnp.asarray(o, jnp.int32) for o in offs])
    chunks = len(halves) * groups * hw // CHUNK
    plan = (len(rows), first, len(halves), groups, piece, hw, width, len(deps) + (out is not None), sub)
    args = [factors, *rows, *[a for h in halves for a in h], *deps]
    hbm = pl.BlockSpec(memory_space=pl.ANY)
    in_specs = [pl.BlockSpec(memory_space=pltpu.VMEM)] + [hbm] * (len(args) - 1)
    aliases = {}
    if out is not None:
        aliases = {len(args) + 1: 0}
        args.append(out)
        in_specs.append(hbm)
    m, n = len(rows) * piece, len(halves) * groups * hw
    return pl.pallas_call(
        lambda *refs: gemm_kernel(plan, *refs),
        out_shape=(jax.ShapeDtypeStruct(out_shape, jnp.float32), jax.ShapeDtypeStruct((8, 128), jnp.float32)),
        grid_spec=pltpu.PrefetchScalarGridSpec(
            num_scalar_prefetch=1,
            grid=(),
            in_specs=in_specs,
            out_specs=(hbm, pl.BlockSpec(memory_space=pltpu.VMEM)),
            scratch_shapes=[
                pltpu.VMEM((m, depth), jnp.bfloat16),
                pltpu.VMEM((chunks, depth, CHUNK), jnp.bfloat16),
                pltpu.VMEM((2, nt * sub, depth), jnp.bfloat16),
                pltpu.VMEM((SLOTS, nt, sub, CHUNK), jnp.float32),
                pltpu.SemaphoreType.DMA((len(rows),)),
                pltpu.SemaphoreType.DMA((len(halves), groups)),
                pltpu.SemaphoreType.DMA((SLOTS, CHUNK // hw)),
            ],
        ),
        input_output_aliases=aliases,
        compiler_params=pltpu.CompilerParams(vmem_limit_bytes=48 * 1024 * 1024),
        cost_estimate=pl.CostEstimate(
            flops=COST * nt * m * n * depth,
            bytes_accessed=4 * nt * m * n + 2 * depth * (m + n),
            transcendentals=0,
        ),
    )(offs, *args)


def solution(mesh):
    R, C = mesh.shape["row"], mesh.shape["col"]
    Z = C // 2

    def on_device(pair_ints, denominators, lap_points, lap_weights):
        depth, width = pair_ints.shape
        r, u = lax.axis_index("row"), lax.axis_index("col")
        z, core = u // 2, lax.rem(u, 2)
        factors = lap_weights[:, None] * jnp.exp(-lap_points[:, None] * denominators[None, :])
        nt = factors.shape[0]
        n_halves = 2 if width % 256 == 0 else 1
        hw = width // n_halves

        perm = [(f, (f % R) * C + f // R) for f in range(R * C)]
        own = [lax.ppermute(pair_ints[:, h * hw : (h + 1) * hw], ("row", "col"), perm) for h in range(n_halves)]

        def row_perm(x, e):
            return lax.ppermute(x, "row", [(a, a ^ e) for a in range(R)])

        halves = [[own[h]] + [row_perm(own[h], e) for e in range(1, R)] for h in range(n_halves)]
        places = [r ^ e for e in range(R)]

        def col_perm(x, pairs):
            return lax.ppermute(x, "col", [(2 * a + k, 2 * b + k) for a, b in pairs for k in range(2)])

        def swap(x):
            return lax.ppermute(x, "col", [(a, a ^ 1) for a in range(C)])

        out_shape = (nt, C * width, R * width)

        def block(x, where, extra, first, hs, out, deps=()):
            offs = [(2 * where + core) * width + extra, (2 * where + 1 - core) * width + extra]
            return gemm(factors, [x[0], x[1]], offs, first, hs, places, out, out_shape, width, deps)

        mine = pair_ints.T
        late = tie(mine, *own)
        out = None
        for h in range(n_halves):
            out, token = block((mine, swap(mine)), z, 0, h, [halves[h]], out, (late,))
        if Z != 4:
            for d in range(1, Z):
                x = col_perm(late, [((a + d) % Z, a) for a in range(Z)])
                out, _ = block((x, swap(x)), lax.rem(z + d, Z), 0, 0, halves, out)
            return out

        up = col_perm(late, [((a + 1) % Z, a) for a in range(Z)])
        down = col_perm(late, [((a - 1) % Z, a) for a in range(Z)])
        fwd = tie(jnp.where(z == 1, up, jnp.where(z == 2, down, late)), token)
        pairs = [(1, 0), (2, 3), (3, 1), (0, 2)]
        m2 = width // 2
        last = [col_perm(fwd[:m2], pairs), col_perm(fwd[m2:], pairs)]
        tokens = []
        for x, d in ((up, 1), (down, Z - 1)):
            out, token = block((x, swap(x)), lax.rem(z + d, Z), 0, 0, halves, out)
            tokens.append(token)
        for k in range(2):
            x = tie(last[k], tokens[k])
            out, _ = block((x, swap(x)), lax.rem(z + 2, Z), k * m2, 0, halves, out)
        return out

    in_specs = (P(None, ("row", "col")), P(), P(), P())
    out_specs = P(None, "row", "col")
    return jax.shard_map(on_device, mesh=mesh, in_specs=in_specs, out_specs=out_specs, check_vma=False)
```

```python
import jax
import jax.numpy as jnp
from jax import lax
from jax.experimental import pallas as pl
from jax.experimental.pallas import tpu as pltpu
from jax.sharding import PartitionSpec as P

CHUNK = 512
SUB = 256
STRIP = 16
SLOTS = 3


def gemm_kernel(plan, offs_ref, fac_ref, *refs):
    sizes, first, n_halves, groups, hw, width, n_more, sub = plan
    refs = list(refs)
    row_refs = [refs.pop(0) for _ in sizes]
    col_refs = [refs.pop(0) for _ in range(n_halves)]
    refs = refs[n_more:]
    out_ref, tok_ref = refs.pop(0), refs.pop(0)
    tok_ref[...] = jnp.zeros_like(tok_ref)
    rows_v, cols_v, w_v, o_v, row_sem, col_sem, out_sem = refs
    nt, depth = fac_ref.shape
    starts = [sum(sizes[:p]) for p in range(len(sizes))]
    per = CHUNK // hw
    per_half = groups // per
    chunks = n_halves * per_half
    subs = sum(sizes) // sub
    part = sub // chunks

    def row_copy(p):
        return pltpu.make_async_copy(row_refs[p], rows_v.at[pl.ds(starts[p], sizes[p])], row_sem.at[p])

    def col_copy(h, g, sem_h, sem_g):
        i = offs_ref[subs + g]
        return pltpu.make_async_copy(
            col_refs[h].at[g],
            cols_v.at[h * per_half + i // per, :, pl.ds(pl.multiple_of(lax.rem(i, per) * hw, hw), hw)],
            col_sem.at[sem_h, sem_g],
        )

    row_copy(0).start()
    for h in range(n_halves):
        for g in range(groups):
            col_copy(h, g, h, g).start()
    for p in range(1, len(sizes)):
        row_copy(p).start()

    def weigh(slot, src, dst):
        x = rows_v[pl.ds(src, STRIP), :].astype(jnp.float32)
        for t in range(nt):
            w_v[slot, pl.ds(t * sub + dst, STRIP), :] = (x * fac_ref[pl.ds(t, 1), :]).astype(jnp.bfloat16)

    row_copy(0).wait()

    def weigh_first(k, _):
        at = pl.multiple_of(k * STRIP, STRIP)
        weigh(0, at, at)
        return 0

    lax.fori_loop(0, sub // STRIP, weigh_first, 0)

    def out_copies(slot, s, n):
        h = n // per_half
        i0 = lax.rem(n, per_half) * per
        row0 = pl.multiple_of(offs_ref[s], sub)
        return [
            pltpu.make_async_copy(
                o_v.at[slot, :, :, pl.ds(e * hw, hw)],
                out_ref.at[:, pl.ds(row0, sub), pl.ds(pl.multiple_of((i0 + e) * width + (first + h) * hw, hw), hw)],
                out_sem.at[slot, e],
            )
            for e in range(per)
        ]

    total = subs * chunks

    def step(q, _):
        s, n = q // chunks, lax.rem(q, chunks)
        slot = lax.rem(q, SLOTS)
        cur = lax.rem(s, 2)

        @pl.when(s == 0)
        def _():
            h = n // per_half
            for e in range(per):
                g = offs_ref[subs + lax.rem(n, per_half) * per + e]
                col_copy(0, 0, h, g).wait()

        for p in range(1, len(sizes)):

            @pl.when((n == 0) & (s + 1 == starts[p] // sub))
            def _():
                row_copy(p).wait()

        @pl.when(q >= SLOTS)
        def _():
            for c in out_copies(slot, s, n):
                c.wait()

        src = jnp.minimum(s + 1, subs - 1) * sub + n * part
        for k in range(part // STRIP):
            weigh(1 - cur, pl.multiple_of(src + k * STRIP, STRIP), pl.multiple_of(n * part + k * STRIP, STRIP))
        res = jnp.dot(w_v[cur], cols_v[n], preferred_element_type=jnp.float32)
        o_v[slot] = res.reshape(nt, sub, CHUNK)
        for c in out_copies(slot, s, n):
            c.start()
        return 0

    lax.fori_loop(0, total, step, 0)
    for q in range(max(0, total - SLOTS), total):
        for c in out_copies(q % SLOTS, q // chunks, q % chunks):
            c.wait()


def tie(x, *deps):
    hbm = pl.BlockSpec(memory_space=pl.ANY)
    return pl.pallas_call(
        lambda *refs: None,
        out_shape=jax.ShapeDtypeStruct(x.shape, x.dtype),
        in_specs=[hbm] * (1 + len(deps)),
        out_specs=hbm,
        input_output_aliases={0: 0},
        compiler_params=pltpu.CompilerParams(vmem_limit_bytes=48 * 1024 * 1024),
    )(x, *deps)


def gemm(factors, rows, row_offs, first, halves, shards, out, out_shape, width, deps=()):
    nt, depth = factors.shape
    sizes = [x.shape[0] for x in rows]
    groups, _, hw = halves[0].shape
    sub = min(SUB, *sizes)
    offs = [o + k * sub for o, m in zip(row_offs, sizes) for k in range(m // sub)] + list(shards)
    offs = jnp.stack([jnp.asarray(o, jnp.int32) for o in offs])
    chunks = len(halves) * groups * hw // CHUNK
    plan = (sizes, first, len(halves), groups, hw, width, len(deps) + (out is not None), sub)
    args = [factors, *rows, *halves, *deps]
    hbm = pl.BlockSpec(memory_space=pl.ANY)
    in_specs = [pl.BlockSpec(memory_space=pltpu.VMEM)] + [hbm] * (len(args) - 1)
    aliases = {}
    if out is not None:
        aliases = {len(args) + 1: 0}
        args.append(out)
        in_specs.append(hbm)
    m, n = sum(sizes), len(halves) * groups * hw
    return pl.pallas_call(
        lambda *refs: gemm_kernel(plan, *refs),
        out_shape=(jax.ShapeDtypeStruct(out_shape, jnp.float32), jax.ShapeDtypeStruct((8, 128), jnp.float32)),
        grid_spec=pltpu.PrefetchScalarGridSpec(
            num_scalar_prefetch=1,
            grid=(),
            in_specs=in_specs,
            out_specs=(hbm, pl.BlockSpec(memory_space=pltpu.VMEM)),
            scratch_shapes=[
                pltpu.VMEM((m, depth), jnp.bfloat16),
                pltpu.VMEM((chunks, depth, CHUNK), jnp.bfloat16),
                pltpu.VMEM((2, nt * sub, depth), jnp.bfloat16),
                pltpu.VMEM((SLOTS, nt, sub, CHUNK), jnp.float32),
                pltpu.SemaphoreType.DMA((len(sizes),)),
                pltpu.SemaphoreType.DMA((len(halves), groups)),
                pltpu.SemaphoreType.DMA((SLOTS, CHUNK // hw)),
            ],
        ),
        input_output_aliases=aliases,
        compiler_params=pltpu.CompilerParams(vmem_limit_bytes=48 * 1024 * 1024),
        cost_estimate=pl.CostEstimate(
            flops=2 * nt * m * n * depth,
            bytes_accessed=4 * nt * m * n + 2 * depth * (m + n),
            transcendentals=0,
        ),
    )(offs, *args)


def solution(mesh):
    R, C = mesh.shape["row"], mesh.shape["col"]
    Z = C // 2
    B = C // R

    def on_device(pair_ints, denominators, lap_points, lap_weights):
        depth, width = pair_ints.shape
        u = lax.axis_index("col")
        z, core = u // 2, lax.rem(u, 2)
        factors = lap_weights[:, None] * jnp.exp(-lap_points[:, None] * denominators[None, :])
        nt = factors.shape[0]
        n_halves = 2 if width % 256 == 0 else 1
        hw = width // n_halves
        out_shape = (nt, C * width, R * width)

        def spread(x):
            return lax.ppermute(x, ("row", "col"), [(a * C + b, (a ^ b % R) * C + b) for a in range(R) for b in range(C)])

        def deliver(x):
            return lax.ppermute(
                x, ("row", "col"), [(a * C + b, a * C + (a ^ b % R) * B + b // R) for a in range(R) for b in range(C)]
            )

        def gather(x):
            return lax.all_gather(x, "row", axis=0)

        def col_perm(x, pairs):
            return lax.ppermute(x, "col", [(2 * a + k, 2 * b + k) for a, b in pairs for k in range(2)])

        def swap(x):
            return lax.ppermute(x, "col", [(a, a ^ 1) for a in range(C)])

        shards = [g ^ (u // B) for g in range(R)]

        def block(pieces, first, hs, out, deps=()):
            rows, offs = [], []
            for x, swapped, where, extra in pieces:
                rows += [x, swapped]
                offs += [(2 * where + core) * width + extra, (2 * where + 1 - core) * width + extra]
            return gemm(factors, rows, offs, first, hs, shards, out, out_shape, width, deps)

        mine = pair_ints.T
        own = (mine, swap(mine), z, 0)
        if Z != 4 or n_halves != 2:
            halves = [gather(deliver(spread(pair_ints[:, h * hw : (h + 1) * hw]))) for h in range(n_halves)]
            out, _ = block([own], 0, halves, None)
            for d in range(1, Z):
                x = col_perm(mine, [((a + d) % Z, a) for a in range(Z)])
                out, _ = block([(x, swap(x), lax.rem(z + d, Z), 0)], 0, halves, out)
            return out

        m2 = width // 2
        nxt = [((a + 1) % Z, a) for a in range(Z)]
        prv = [((a - 1) % Z, a) for a in range(Z)]
        up_a = col_perm(mine[:m2], nxt)
        sent_a = spread(pair_ints[:, :hw])
        sent_b = spread(tie(pair_ints[:, hw:], sent_a))
        got_a = deliver(tie(sent_a, up_a))
        got_b = deliver(sent_b)
        cols_a, cols_b = gather(got_a), gather(got_b)
        late = tie(mine, got_a)
        up_b = col_perm(late[m2:], nxt)
        late = tie(late, got_b)
        down = col_perm(late, prv)

        one = lax.rem(z + 1, Z)
        ups = [(up_a, swap(up_a), one, 0), (up_b, swap(up_b), one, m2)]
        out, token = block([own], 0, [cols_a], None, (late,))
        out, token = block(ups, 0, [cols_a], out)
        up = jnp.concatenate([up_a, up_b])
        down = tie(down, token)
        fwd = jnp.where(z == 1, up, jnp.where(z == 2, down, late))
        pairs = [(1, 0), (2, 3), (3, 1), (0, 2)]
        last = [col_perm(fwd[:m2], pairs), col_perm(fwd[m2:], pairs)]
        out, token_b = block([own] + ups, 1, [cols_b], out, (fwd,))
        halves = [cols_a, cols_b]
        out, token_d = block([(down, swap(down), lax.rem(z + 3, Z), 0)], 0, halves, out)
        for k, token in enumerate((token_b, token_d)):
            x = tie(last[k], token)
            out, _ = block([(x, swap(x), lax.rem(z + 2, Z), k * m2)], 0, halves, out)
        return out

    in_specs = (P(None, ("row", "col")), P(), P(), P())
    out_specs = P(None, "row", "col")
    return jax.shard_map(on_device, mesh=mesh, in_specs=in_specs, out_specs=out_specs, check_vma=False)
```

```python
import jax
import jax.numpy as jnp
from jax import lax
from jax.experimental import pallas as pl
from jax.experimental.pallas import tpu as pltpu
from jax.sharding import PartitionSpec as P

CHUNK = 1024
SUB = 512
STRIP = 16
SLOTS = 2


def gemm_kernel(plan, offs_ref, fac_ref, *refs):
    sizes, first, n_halves, groups, hw, width, n_more, sub = plan
    refs = list(refs)
    row_refs = [refs.pop(0) for _ in sizes]
    col_refs = [refs.pop(0) for _ in range(n_halves)]
    refs = refs[n_more:]
    out_ref, tok_ref = refs.pop(0), refs.pop(0)
    tok_ref[...] = jnp.zeros_like(tok_ref)
    rows_v, cols_v, w_v, o_v, row_sem, col_sem, out_sem = refs
    nt, depth = fac_ref.shape
    starts = [sum(sizes[:p]) for p in range(len(sizes))]
    per = CHUNK // hw
    per_half = groups // per
    chunks = n_halves * per_half
    subs = sum(sizes) // sub
    part = sub // chunks

    def row_copy(p):
        return pltpu.make_async_copy(row_refs[p], rows_v.at[pl.ds(starts[p], sizes[p])], row_sem.at[p])

    def col_copy(h, g, sem_h, sem_g):
        i = offs_ref[subs + g]
        return pltpu.make_async_copy(
            col_refs[h].at[g],
            cols_v.at[h * per_half + i // per, :, pl.ds(pl.multiple_of(lax.rem(i, per) * hw, hw), hw)],
            col_sem.at[sem_h, sem_g],
        )

    row_copy(0).start()
    for h in range(n_halves):
        for g in range(groups):
            col_copy(h, g, h, g).start()
    for p in range(1, len(sizes)):
        row_copy(p).start()

    def weigh(slot, src, dst):
        x = rows_v[pl.ds(src, STRIP), :].astype(jnp.float32)
        for t in range(nt):
            w_v[slot, pl.ds(t * sub + dst, STRIP), :] = (x * fac_ref[pl.ds(t, 1), :]).astype(jnp.bfloat16)

    row_copy(0).wait()

    def weigh_first(k, _):
        at = pl.multiple_of(k * STRIP, STRIP)
        weigh(0, at, at)
        return 0

    lax.fori_loop(0, sub // STRIP, weigh_first, 0)

    def out_copies(slot, s, n):
        h = n // per_half
        i0 = lax.rem(n, per_half) * per
        row0 = pl.multiple_of(offs_ref[s], sub)
        return [
            pltpu.make_async_copy(
                o_v.at[slot, :, :, pl.ds(e * hw, hw)],
                out_ref.at[:, pl.ds(row0, sub), pl.ds(pl.multiple_of((i0 + e) * width + (first + h) * hw, hw), hw)],
                out_sem.at[slot, e],
            )
            for e in range(per)
        ]

    total = subs * chunks

    def step(q, _):
        s, n = q // chunks, lax.rem(q, chunks)
        slot = lax.rem(q, SLOTS)
        cur = lax.rem(s, 2)

        @pl.when(s == 0)
        def _():
            h = n // per_half
            for e in range(per):
                g = offs_ref[subs + lax.rem(n, per_half) * per + e]
                col_copy(0, 0, h, g).wait()

        for p in range(1, len(sizes)):

            @pl.when((n == 0) & (s + 1 == starts[p] // sub))
            def _():
                row_copy(p).wait()

        @pl.when(q >= SLOTS)
        def _():
            for c in out_copies(slot, s, n):
                c.wait()

        src = jnp.minimum(s + 1, subs - 1) * sub + n * part
        for k in range(part // STRIP):
            weigh(1 - cur, pl.multiple_of(src + k * STRIP, STRIP), pl.multiple_of(n * part + k * STRIP, STRIP))
        res = jnp.dot(w_v[cur], cols_v[n], preferred_element_type=jnp.float32)
        o_v[slot] = res.reshape(nt, sub, CHUNK)
        for c in out_copies(slot, s, n):
            c.start()
        return 0

    lax.fori_loop(0, total, step, 0)
    for q in range(max(0, total - SLOTS), total):
        for c in out_copies(q % SLOTS, q // chunks, q % chunks):
            c.wait()


def tie(x, *deps):
    hbm = pl.BlockSpec(memory_space=pl.ANY)
    return pl.pallas_call(
        lambda *refs: None,
        out_shape=jax.ShapeDtypeStruct(x.shape, x.dtype),
        in_specs=[hbm] * (1 + len(deps)),
        out_specs=hbm,
        input_output_aliases={0: 0},
        compiler_params=pltpu.CompilerParams(vmem_limit_bytes=54 * 1024 * 1024),
    )(x, *deps)


def gemm(factors, rows, row_offs, first, halves, shards, out, out_shape, width, deps=()):
    nt, depth = factors.shape
    sizes = [x.shape[0] for x in rows]
    groups, _, hw = halves[0].shape
    sub = min(SUB, *sizes)
    offs = [o + k * sub for o, m in zip(row_offs, sizes) for k in range(m // sub)] + list(shards)
    offs = jnp.stack([jnp.asarray(o, jnp.int32) for o in offs])
    chunks = len(halves) * groups * hw // CHUNK
    plan = (sizes, first, len(halves), groups, hw, width, len(deps) + (out is not None), sub)
    args = [factors, *rows, *halves, *deps]
    hbm = pl.BlockSpec(memory_space=pl.ANY)
    in_specs = [pl.BlockSpec(memory_space=pltpu.VMEM)] + [hbm] * (len(args) - 1)
    aliases = {}
    if out is not None:
        aliases = {len(args) + 1: 0}
        args.append(out)
        in_specs.append(hbm)
    m, n = sum(sizes), len(halves) * groups * hw
    return pl.pallas_call(
        lambda *refs: gemm_kernel(plan, *refs),
        out_shape=(jax.ShapeDtypeStruct(out_shape, jnp.float32), jax.ShapeDtypeStruct((8, 128), jnp.float32)),
        grid_spec=pltpu.PrefetchScalarGridSpec(
            num_scalar_prefetch=1,
            grid=(),
            in_specs=in_specs,
            out_specs=(hbm, pl.BlockSpec(memory_space=pltpu.VMEM)),
            scratch_shapes=[
                pltpu.VMEM((m, depth), jnp.bfloat16),
                pltpu.VMEM((chunks, depth, CHUNK), jnp.bfloat16),
                pltpu.VMEM((2, nt * sub, depth), jnp.bfloat16),
                pltpu.VMEM((SLOTS, nt, sub, CHUNK), jnp.float32),
                pltpu.SemaphoreType.DMA((len(sizes),)),
                pltpu.SemaphoreType.DMA((len(halves), groups)),
                pltpu.SemaphoreType.DMA((SLOTS, CHUNK // hw)),
            ],
        ),
        input_output_aliases=aliases,
        compiler_params=pltpu.CompilerParams(vmem_limit_bytes=54 * 1024 * 1024),
        cost_estimate=pl.CostEstimate(
            flops=2 * nt * m * n * depth,
            bytes_accessed=4 * nt * m * n + 2 * depth * (m + n),
            transcendentals=0,
        ),
    )(offs, *args)


def solution(mesh):
    R, C = mesh.shape["row"], mesh.shape["col"]
    Z = C // 2
    B = C // R

    def on_device(pair_ints, denominators, lap_points, lap_weights):
        depth, width = pair_ints.shape
        u = lax.axis_index("col")
        z, core = u // 2, lax.rem(u, 2)
        factors = lap_weights[:, None] * jnp.exp(-lap_points[:, None] * denominators[None, :])
        nt = factors.shape[0]
        n_halves = 2 if width % 256 == 0 else 1
        hw = width // n_halves
        out_shape = (nt, C * width, R * width)

        def spread(x):
            return lax.ppermute(x, ("row", "col"), [(a * C + b, (a ^ b % R) * C + b) for a in range(R) for b in range(C)])

        def deliver(x):
            return lax.ppermute(
                x, ("row", "col"), [(a * C + b, a * C + (a ^ b % R) * B + b // R) for a in range(R) for b in range(C)]
            )

        def gather(x):
            return lax.all_gather(x, "row", axis=0)

        def col_perm(x, pairs):
            return lax.ppermute(x, "col", [(2 * a + k, 2 * b + k) for a, b in pairs for k in range(2)])

        def swap(x):
            return lax.ppermute(x, "col", [(a, a ^ 1) for a in range(C)])

        shards = [g ^ (u // B) for g in range(R)]

        def block(pieces, first, hs, out, deps=()):
            rows, offs = [], []
            for x, swapped, where, extra in pieces:
                rows += [x, swapped]
                offs += [(2 * where + core) * width + extra, (2 * where + 1 - core) * width + extra]
            return gemm(factors, rows, offs, first, hs, shards, out, out_shape, width, deps)

        mine = pair_ints.T
        own = (mine, swap(mine), z, 0)
        if Z != 4 or n_halves != 2:
            halves = [gather(deliver(spread(pair_ints[:, h * hw : (h + 1) * hw]))) for h in range(n_halves)]
            out, _ = block([own], 0, halves, None)
            for d in range(1, Z):
                x = col_perm(mine, [((a + d) % Z, a) for a in range(Z)])
                out, _ = block([(x, swap(x), lax.rem(z + d, Z), 0)], 0, halves, out)
            return out

        up = col_perm(mine, [((a + 1) % Z, a) for a in range(Z)])
        sent_a = spread(pair_ints[:, :hw])
        sent_b = spread(pair_ints[:, hw:])
        got_a = deliver(tie(sent_a, sent_b, up))
        got_b = deliver(tie(sent_b, got_a))
        late = tie(mine, got_a)
        down = col_perm(late, [((a - 1) % Z, a) for a in range(Z)])
        cols_a, cols_b = gather(got_a), gather(got_b)

        ups = (up, swap(up), lax.rem(z + 1, Z), 0)
        out, token = block([own], 0, [cols_a], None, (late, got_b))
        down = tie(down, token)
        fwd = jnp.where(z == 1, up, jnp.where(z == 2, down, late))
        last = col_perm(fwd, [(1, 0), (2, 3), (3, 1), (0, 2)])
        downs = (down, swap(down), lax.rem(z + 3, Z), 0)
        out, token = block([ups], 0, [cols_a], out, (fwd,))
        out, token = block([downs], 0, [cols_a], out)
        out, token = block([own, ups], 1, [cols_b], out, (token,))
        last = tie(last, token)
        out, token = block([downs], 1, [cols_b], out)
        out, token = block([(last, swap(last), lax.rem(z + 2, Z), 0)], 0, [cols_a, cols_b], out)
        return out

    in_specs = (P(None, ("row", "col")), P(), P(), P())
    out_specs = P(None, "row", "col")
    return jax.shard_map(on_device, mesh=mesh, in_specs=in_specs, out_specs=out_specs, check_vma=False)
```

```python
import jax
import jax.numpy as jnp
from jax import lax
from jax.experimental import pallas as pl
from jax.experimental.pallas import tpu as pltpu
from jax.sharding import PartitionSpec as P

CHUNK = 512
SUB = 256
STRIP = 16
SLOTS = 3


def gemm_kernel(plan, offs_ref, fac_ref, *refs):
    sizes, first, n_halves, groups, hw, width, n_more, sub = plan
    refs = list(refs)
    row_refs = [refs.pop(0) for _ in sizes]
    col_refs = [refs.pop(0) for _ in range(n_halves)]
    refs = refs[n_more:]
    out_ref, tok_ref = refs.pop(0), refs.pop(0)
    tok_ref[...] = jnp.zeros_like(tok_ref)
    rows_v, cols_v, w_v, o_v, row_sem, col_sem, out_sem = refs
    nt, depth = fac_ref.shape
    starts = [sum(sizes[:p]) for p in range(len(sizes))]
    per = CHUNK // hw
    per_half = groups // per
    chunks = n_halves * per_half
    subs = sum(sizes) // sub
    part = sub // chunks

    def row_copy(p):
        return pltpu.make_async_copy(row_refs[p], rows_v.at[pl.ds(starts[p], sizes[p])], row_sem.at[p])

    def col_copy(h, g, sem_h, sem_g):
        i = offs_ref[subs + g]
        return pltpu.make_async_copy(
            col_refs[h].at[g],
            cols_v.at[h * per_half + i // per, :, pl.ds(pl.multiple_of(lax.rem(i, per) * hw, hw), hw)],
            col_sem.at[sem_h, sem_g],
        )

    row_copy(0).start()
    for h in range(n_halves):
        for g in range(groups):
            col_copy(h, g, h, g).start()
    for p in range(1, len(sizes)):
        row_copy(p).start()

    def weigh(slot, src, dst):
        x = rows_v[pl.ds(src, STRIP), :].astype(jnp.float32)
        for t in range(nt):
            w_v[slot, pl.ds(t * sub + dst, STRIP), :] = (x * fac_ref[pl.ds(t, 1), :]).astype(jnp.bfloat16)

    row_copy(0).wait()

    def weigh_first(k, _):
        at = pl.multiple_of(k * STRIP, STRIP)
        weigh(0, at, at)
        return 0

    lax.fori_loop(0, sub // STRIP, weigh_first, 0)

    def out_copies(slot, s, n):
        h = n // per_half
        i0 = lax.rem(n, per_half) * per
        row0 = pl.multiple_of(offs_ref[s], sub)
        return [
            pltpu.make_async_copy(
                o_v.at[slot, :, :, pl.ds(e * hw, hw)],
                out_ref.at[:, pl.ds(row0, sub), pl.ds(pl.multiple_of((i0 + e) * width + (first + h) * hw, hw), hw)],
                out_sem.at[slot, e],
            )
            for e in range(per)
        ]

    total = subs * chunks

    def step(q, _):
        s, n = q // chunks, lax.rem(q, chunks)
        slot = lax.rem(q, SLOTS)
        cur = lax.rem(s, 2)

        @pl.when(s == 0)
        def _():
            h = n // per_half
            for e in range(per):
                g = offs_ref[subs + lax.rem(n, per_half) * per + e]
                col_copy(0, 0, h, g).wait()

        for p in range(1, len(sizes)):

            @pl.when((n == 0) & (s + 1 == starts[p] // sub))
            def _():
                row_copy(p).wait()

        @pl.when(q >= SLOTS)
        def _():
            for c in out_copies(slot, s, n):
                c.wait()

        src = jnp.minimum(s + 1, subs - 1) * sub + n * part
        for k in range(part // STRIP):
            weigh(1 - cur, pl.multiple_of(src + k * STRIP, STRIP), pl.multiple_of(n * part + k * STRIP, STRIP))
        res = jnp.dot(w_v[cur], cols_v[n], preferred_element_type=jnp.float32)
        o_v[slot] = res.reshape(nt, sub, CHUNK)
        for c in out_copies(slot, s, n):
            c.start()
        return 0

    lax.fori_loop(0, total, step, 0)
    for q in range(max(0, total - SLOTS), total):
        for c in out_copies(q % SLOTS, q // chunks, q % chunks):
            c.wait()


def tie(x, *deps):
    hbm = pl.BlockSpec(memory_space=pl.ANY)
    return pl.pallas_call(
        lambda *refs: None,
        out_shape=jax.ShapeDtypeStruct(x.shape, x.dtype),
        in_specs=[hbm] * (1 + len(deps)),
        out_specs=hbm,
        input_output_aliases={0: 0},
        compiler_params=pltpu.CompilerParams(vmem_limit_bytes=54 * 1024 * 1024),
    )(x, *deps)


def gemm(factors, rows, row_offs, first, halves, shards, out, out_shape, width, deps=()):
    nt, depth = factors.shape
    sizes = [x.shape[0] for x in rows]
    groups, _, hw = halves[0].shape
    sub = min(SUB, *sizes)
    offs = [o + k * sub for o, m in zip(row_offs, sizes) for k in range(m // sub)] + list(shards)
    offs = jnp.stack([jnp.asarray(o, jnp.int32) for o in offs])
    chunks = len(halves) * groups * hw // CHUNK
    plan = (sizes, first, len(halves), groups, hw, width, len(deps) + (out is not None), sub)
    args = [factors, *rows, *halves, *deps]
    hbm = pl.BlockSpec(memory_space=pl.ANY)
    in_specs = [pl.BlockSpec(memory_space=pltpu.VMEM)] + [hbm] * (len(args) - 1)
    aliases = {}
    if out is not None:
        aliases = {len(args) + 1: 0}
        args.append(out)
        in_specs.append(hbm)
    m, n = sum(sizes), len(halves) * groups * hw
    return pl.pallas_call(
        lambda *refs: gemm_kernel(plan, *refs),
        out_shape=(jax.ShapeDtypeStruct(out_shape, jnp.float32), jax.ShapeDtypeStruct((8, 128), jnp.float32)),
        grid_spec=pltpu.PrefetchScalarGridSpec(
            num_scalar_prefetch=1,
            grid=(),
            in_specs=in_specs,
            out_specs=(hbm, pl.BlockSpec(memory_space=pltpu.VMEM)),
            scratch_shapes=[
                pltpu.VMEM((m, depth), jnp.bfloat16),
                pltpu.VMEM((chunks, depth, CHUNK), jnp.bfloat16),
                pltpu.VMEM((2, nt * sub, depth), jnp.bfloat16),
                pltpu.VMEM((SLOTS, nt, sub, CHUNK), jnp.float32),
                pltpu.SemaphoreType.DMA((len(sizes),)),
                pltpu.SemaphoreType.DMA((len(halves), groups)),
                pltpu.SemaphoreType.DMA((SLOTS, CHUNK // hw)),
            ],
        ),
        input_output_aliases=aliases,
        compiler_params=pltpu.CompilerParams(vmem_limit_bytes=54 * 1024 * 1024),
        cost_estimate=pl.CostEstimate(
            flops=2 * nt * m * n * depth,
            bytes_accessed=4 * nt * m * n + 2 * depth * (m + n),
            transcendentals=0,
        ),
    )(offs, *args)


def solution(mesh):
    R, C = mesh.shape["row"], mesh.shape["col"]
    Z = C // 2
    B = C // R

    def on_device(pair_ints, denominators, lap_points, lap_weights):
        depth, width = pair_ints.shape
        u = lax.axis_index("col")
        z, core = u // 2, lax.rem(u, 2)
        factors = lap_weights[:, None] * jnp.exp(-lap_points[:, None] * denominators[None, :])
        nt = factors.shape[0]
        hw = min(128, width)
        n_halves = width // hw
        out_shape = (nt, C * width, R * width)

        def spread(x):
            return lax.ppermute(x, ("row", "col"), [(a * C + b, (a ^ b % R) * C + b) for a in range(R) for b in range(C)])

        def deliver(x):
            return lax.ppermute(
                x, ("row", "col"), [(a * C + b, a * C + (a ^ b % R) * B + b // R) for a in range(R) for b in range(C)]
            )

        def gather(x):
            return lax.all_gather(x, "row", axis=0)

        def col_perm(x, pairs):
            return lax.ppermute(x, "col", [(2 * a + k, 2 * b + k) for a, b in pairs for k in range(2)])

        def swap(x):
            return lax.ppermute(x, "col", [(a, a ^ 1) for a in range(C)])

        shards = [g ^ (u // B) for g in range(R)]

        def block(pieces, first, hs, out, deps=()):
            rows, offs = [], []
            for x, swapped, where, extra in pieces:
                rows += [x, swapped]
                offs += [(2 * where + core) * width + extra, (2 * where + 1 - core) * width + extra]
            return gemm(factors, rows, offs, first, hs, shards, out, out_shape, width, deps)

        mine = pair_ints.T
        own = (mine, swap(mine), z, 0)
        if Z != 4 or n_halves != 4:
            halves = [gather(deliver(spread(pair_ints[:, h * hw : (h + 1) * hw]))) for h in range(n_halves)]
            out, _ = block([own], 0, halves, None)
            for d in range(1, Z):
                x = col_perm(mine, [((a + d) % Z, a) for a in range(Z)])
                out, _ = block([(x, swap(x), lax.rem(z + d, Z), 0)], 0, halves, out)
            return out

        up = col_perm(mine, [((a + 1) % Z, a) for a in range(Z)])
        sent_a = spread(pair_ints[:, : 2 * hw])
        sent_b = spread(pair_ints[:, 2 * hw :])
        got_a = deliver(sent_a)
        got_b = deliver(tie(sent_b, got_a, up))
        late = tie(mine, got_a)
        down = col_perm(late, [((a - 1) % Z, a) for a in range(Z)])
        cols = [gather(x[:, k * hw : (k + 1) * hw]) for x in (got_a, got_b) for k in range(2)]

        ups = (up, swap(up), lax.rem(z + 1, Z), 0)
        out, token = block([own, ups], 0, cols[:1], None, (late,))
        out, token = block([own, ups], 1, cols[1:2], out)
        down = tie(down, token)
        fwd = jnp.where(z == 1, up, jnp.where(z == 2, down, late))
        last = col_perm(fwd, [(1, 0), (2, 3), (3, 1), (0, 2)])
        downs = (down, swap(down), lax.rem(z + 3, Z), 0)
        out, token = block([downs], 0, cols[:2], out, (fwd,))
        out, token = block([own, ups, downs], 2, cols[2:], out)
        last = tie(last, token)
        out, token = block([(last, swap(last), lax.rem(z + 2, Z), 0)], 0, cols, out)
        return out

    in_specs = (P(None, ("row", "col")), P(), P(), P())
    out_specs = P(None, "row", "col")
    return jax.shard_map(on_device, mesh=mesh, in_specs=in_specs, out_specs=out_specs, check_vma=False)
```

```python
import jax
import jax.numpy as jnp
from jax import lax
from jax.experimental import pallas as pl
from jax.experimental.pallas import tpu as pltpu
from jax.sharding import PartitionSpec as P

CHUNK = 512
SUB = 256
STRIP = 16
SLOTS = 3


def gemm_kernel(plan, offs_ref, fac_ref, *refs):
    sizes, first, n_halves, groups, hw, width, n_more, sub = plan
    refs = list(refs)
    row_refs = [refs.pop(0) for _ in sizes]
    col_refs = [refs.pop(0) for _ in range(n_halves)]
    refs = refs[n_more:]
    out_ref, tok_ref = refs.pop(0), refs.pop(0)
    tok_ref[...] = jnp.zeros_like(tok_ref)
    rows_v, cols_v, w_v, o_v, row_sem, col_sem, out_sem = refs
    nt, depth = fac_ref.shape
    starts = [sum(sizes[:p]) for p in range(len(sizes))]
    per = CHUNK // hw
    per_half = groups // per
    chunks = n_halves * per_half
    subs = sum(sizes) // sub
    part = sub // chunks

    def row_copy(p):
        return pltpu.make_async_copy(row_refs[p], rows_v.at[pl.ds(starts[p], sizes[p])], row_sem.at[p])

    def col_copy(h, g, sem_h, sem_g):
        i = offs_ref[subs + g]
        return pltpu.make_async_copy(
            col_refs[h].at[g],
            cols_v.at[h * per_half + i // per, :, pl.ds(pl.multiple_of(lax.rem(i, per) * hw, hw), hw)],
            col_sem.at[sem_h, sem_g],
        )

    row_copy(0).start()
    for h in range(n_halves):
        for g in range(groups):
            col_copy(h, g, h, g).start()
    for p in range(1, len(sizes)):
        row_copy(p).start()

    def weigh(slot, src, dst):
        x = rows_v[pl.ds(src, STRIP), :].astype(jnp.float32)
        for t in range(nt):
            w_v[slot, pl.ds(t * sub + dst, STRIP), :] = (x * fac_ref[pl.ds(t, 1), :]).astype(jnp.bfloat16)

    row_copy(0).wait()

    def weigh_first(k, _):
        at = pl.multiple_of(k * STRIP, STRIP)
        weigh(0, at, at)
        return 0

    lax.fori_loop(0, sub // STRIP, weigh_first, 0)

    def out_copies(slot, s, n):
        h = n // per_half
        i0 = lax.rem(n, per_half) * per
        row0 = pl.multiple_of(offs_ref[s], sub)
        return [
            pltpu.make_async_copy(
                o_v.at[slot, :, :, pl.ds(e * hw, hw)],
                out_ref.at[:, pl.ds(row0, sub), pl.ds(pl.multiple_of((i0 + e) * width + (first + h) * hw, hw), hw)],
                out_sem.at[slot, e],
            )
            for e in range(per)
        ]

    total = subs * chunks

    def step(q, _):
        s, n = q // chunks, lax.rem(q, chunks)
        slot = lax.rem(q, SLOTS)
        cur = lax.rem(s, 2)

        @pl.when(s == 0)
        def _():
            h = n // per_half
            for e in range(per):
                g = offs_ref[subs + lax.rem(n, per_half) * per + e]
                col_copy(0, 0, h, g).wait()

        for p in range(1, len(sizes)):

            @pl.when((n == 0) & (s + 1 == starts[p] // sub))
            def _():
                row_copy(p).wait()

        @pl.when(q >= SLOTS)
        def _():
            for c in out_copies(slot, s, n):
                c.wait()

        src = jnp.minimum(s + 1, subs - 1) * sub + n * part
        for k in range(part // STRIP):
            weigh(1 - cur, pl.multiple_of(src + k * STRIP, STRIP), pl.multiple_of(n * part + k * STRIP, STRIP))
        res = jnp.dot(w_v[cur], cols_v[n], preferred_element_type=jnp.float32)
        o_v[slot] = res.reshape(nt, sub, CHUNK)
        for c in out_copies(slot, s, n):
            c.start()
        return 0

    lax.fori_loop(0, total, step, 0)
    for q in range(max(0, total - SLOTS), total):
        for c in out_copies(q % SLOTS, q // chunks, q % chunks):
            c.wait()


def tie(x, *deps):
    hbm = pl.BlockSpec(memory_space=pl.ANY)
    return pl.pallas_call(
        lambda *refs: None,
        out_shape=jax.ShapeDtypeStruct(x.shape, x.dtype),
        in_specs=[hbm] * (1 + len(deps)),
        out_specs=hbm,
        input_output_aliases={0: 0},
        compiler_params=pltpu.CompilerParams(vmem_limit_bytes=54 * 1024 * 1024),
    )(x, *deps)


def gemm(factors, rows, row_offs, first, halves, shards, out, out_shape, width, deps=()):
    nt, depth = factors.shape
    sizes = [x.shape[0] for x in rows]
    groups, _, hw = halves[0].shape
    sub = min(SUB, *sizes)
    offs = [o + k * sub for o, m in zip(row_offs, sizes) for k in range(m // sub)] + list(shards)
    offs = jnp.stack([jnp.asarray(o, jnp.int32) for o in offs])
    chunks = len(halves) * groups * hw // CHUNK
    plan = (sizes, first, len(halves), groups, hw, width, len(deps) + (out is not None), sub)
    args = [factors, *rows, *halves, *deps]
    hbm = pl.BlockSpec(memory_space=pl.ANY)
    in_specs = [pl.BlockSpec(memory_space=pltpu.VMEM)] + [hbm] * (len(args) - 1)
    aliases = {}
    if out is not None:
        aliases = {len(args) + 1: 0}
        args.append(out)
        in_specs.append(hbm)
    m, n = sum(sizes), len(halves) * groups * hw
    return pl.pallas_call(
        lambda *refs: gemm_kernel(plan, *refs),
        out_shape=(jax.ShapeDtypeStruct(out_shape, jnp.float32), jax.ShapeDtypeStruct((8, 128), jnp.float32)),
        grid_spec=pltpu.PrefetchScalarGridSpec(
            num_scalar_prefetch=1,
            grid=(),
            in_specs=in_specs,
            out_specs=(hbm, pl.BlockSpec(memory_space=pltpu.VMEM)),
            scratch_shapes=[
                pltpu.VMEM((m, depth), jnp.bfloat16),
                pltpu.VMEM((chunks, depth, CHUNK), jnp.bfloat16),
                pltpu.VMEM((2, nt * sub, depth), jnp.bfloat16),
                pltpu.VMEM((SLOTS, nt, sub, CHUNK), jnp.float32),
                pltpu.SemaphoreType.DMA((len(sizes),)),
                pltpu.SemaphoreType.DMA((len(halves), groups)),
                pltpu.SemaphoreType.DMA((SLOTS, CHUNK // hw)),
            ],
        ),
        input_output_aliases=aliases,
        compiler_params=pltpu.CompilerParams(vmem_limit_bytes=54 * 1024 * 1024),
        cost_estimate=pl.CostEstimate(
            flops=2 * nt * m * n * depth,
            bytes_accessed=4 * nt * m * n + 2 * depth * (m + n),
            transcendentals=0,
        ),
    )(offs, *args)


def solution(mesh):
    R, C = mesh.shape["row"], mesh.shape["col"]
    Z = C // 2
    B = C // R

    def on_device(pair_ints, denominators, lap_points, lap_weights):
        depth, width = pair_ints.shape
        u = lax.axis_index("col")
        z, core = u // 2, lax.rem(u, 2)
        factors = lap_weights[:, None] * jnp.exp(-lap_points[:, None] * denominators[None, :])
        nt = factors.shape[0]
        n_halves = 2 if width % 256 == 0 else 1
        hw = width // n_halves
        out_shape = (nt, C * width, R * width)

        def spread(x):
            return lax.ppermute(x, ("row", "col"), [(a * C + b, (a ^ b % R) * C + b) for a in range(R) for b in range(C)])

        def deliver(x):
            return lax.ppermute(
                x, ("row", "col"), [(a * C + b, a * C + (a ^ b % R) * B + b // R) for a in range(R) for b in range(C)]
            )

        def gather(x):
            return lax.all_gather(x, "row", axis=0)

        def col_perm(x, pairs):
            return lax.ppermute(x, "col", [(2 * a + k, 2 * b + k) for a, b in pairs for k in range(2)])

        def swap(x):
            return lax.ppermute(x, "col", [(a, a ^ 1) for a in range(C)])

        shards = [g ^ (u // B) for g in range(R)]

        def block(pieces, first, hs, out, deps=()):
            rows, offs = [], []
            for x, swapped, where, extra in pieces:
                rows += [x, swapped]
                offs += [(2 * where + core) * width + extra, (2 * where + 1 - core) * width + extra]
            return gemm(factors, rows, offs, first, hs, shards, out, out_shape, width, deps)

        mine = pair_ints.T
        own = (mine, swap(mine), z, 0)
        if Z != 4 or n_halves != 2:
            halves = [gather(deliver(spread(pair_ints[:, h * hw : (h + 1) * hw]))) for h in range(n_halves)]
            out, _ = block([own], 0, halves, None)
            for d in range(1, Z):
                x = col_perm(mine, [((a + d) % Z, a) for a in range(Z)])
                out, _ = block([(x, swap(x), lax.rem(z + d, Z), 0)], 0, halves, out)
            return out

        up = col_perm(mine, [((a + 1) % Z, a) for a in range(Z)])
        sent_a = spread(pair_ints[:, :hw])
        sent_b = spread(pair_ints[:, hw:])
        got_a = deliver(tie(sent_a, sent_b, up))
        got_b = deliver(tie(sent_b, got_a))
        late = tie(mine, got_a)
        down = col_perm(late, [((a - 1) % Z, a) for a in range(Z)])
        cols_a, cols_b = gather(got_a), gather(got_b)

        ups = (up, swap(up), lax.rem(z + 1, Z), 0)
        out, token = block([own], 0, [cols_a], None, (late, got_b))
        down = tie(down, token)
        fwd = jnp.where(z == 1, up, jnp.where(z == 2, down, late))
        last = col_perm(fwd, [(1, 0), (2, 3), (3, 1), (0, 2)])
        downs = (down, swap(down), lax.rem(z + 3, Z), 0)
        out, token = block([ups], 0, [cols_a], out, (fwd,))
        halves = [cols_a, cols_b]
        out, token = block([downs], 0, halves, out)
        last = tie(last, token)
        out, token = block([own, ups], 1, [cols_b], out)
        out, token = block([(last, swap(last), lax.rem(z + 2, Z), 0)], 0, halves, out)
        return out

    in_specs = (P(None, ("row", "col")), P(), P(), P())
    out_specs = P(None, "row", "col")
    return jax.shard_map(on_device, mesh=mesh, in_specs=in_specs, out_specs=out_specs, check_vma=False)
```
